32 devices in a mesh: req: 8 (over z, x), tp: 4 (over y, core).
Axes of the slice: x: 2, y: 2, z: 4, core: 2. Of those that a mesh axis runs over, the one named last changes fastest.
Arguments:
- queries: bfloat16 [512, 8192], P('req', 'tp'), may hold values from -5 to 5
- key_cache: bfloat16 [512, 64, 1024], P('req', None, 'tp'), may hold values from -5 to 5
- value_cache: bfloat16 [512, 64, 1024], P('req', None, 'tp'), may hold values from -5 to 5
- lengths: int32 [512], P('req'), may hold values from 8 to 64, as said below
- row_adapter_index: int32 [512], replicated, may hold values from 0 to 255, as said below
- down_weight: bfloat16 [256, 8192, 64], P('req', 'tp'), may hold values from -0.0625 to 0.0625
- up_weight: bfloat16 [256, 64, 8192], P('req', None, 'tp'), may hold values from -1.5 to 1.5
Outputs:
- attn_out: bfloat16 [512, 8192], P('req', 'tp')
- adapter_output: bfloat16 [512, 8192], P('req', 'tp')
The draws below stay inside these ranges and needn't reach their ends.
Inputs may be any that keep to these rules, and one draw needn't show every extreme that they name: `row_adapter_index`: adapter a belongs to owner a // 32, the index of req that holds it. Among the 64 rows of one index of req (aligned blocks of the row dimension), at most 8 name adapters of one owner; some owner receives exactly 8 rows from every block. `lengths`: every index of req holds a row of length 64.
All inputs are finite; a program needn't handle non-finite values.
Results may differ from the reference program's by a relative error of at most 0.019.
Values may be sent and summed in bfloat16 or wider, within the bound.
A program may use at most 64 MiB of HBM per device.

```python
import jax
import jax.numpy as jnp
from jax import lax

MODEL_WIDTH = 8192
HEADS = 64
KV_HEADS = 8
HEAD_DIM = 128
ADAPTER_RANK = 64
CAP = 8
ROWS_PER_INDEX = 64
CTX = 64
ADP_REQ = 32
GROUP = 8
REQUEST_ROWS = 512
ADAPTER_TOTAL = 256
N_REQ = 8


def query_key_parts(key):
    key_q, key_k = jax.random.split(key, 2)
    width_kv = KV_HEADS * HEAD_DIM
    queries = jnp.clip(jax.random.normal(key_q, (REQUEST_ROWS, HEADS * HEAD_DIM), jnp.float32), -5.0, 5.0)
    keys = jnp.clip(jax.random.normal(key_k, (REQUEST_ROWS, CTX, width_kv), jnp.float32), -5.0, 5.0)
    return (queries, keys)


def draw_queries(key, part):
    return query_key_parts(jax.random.fold_in(key, 11))[0].astype(jnp.bfloat16)


def draw_key_cache(key, part):
    return query_key_parts(jax.random.fold_in(key, 11))[1].astype(jnp.bfloat16)


def draw_lengths(key, part):
    key_a, key_b, key_c = jax.random.split(key, 3)
    first = jax.random.randint(key_a, (REQUEST_ROWS,), 0, CTX - 7)
    second = jax.random.randint(key_b, (REQUEST_ROWS,), 0, CTX - 7)
    lengths = 8 + first * second // (CTX - 8)
    longest = jax.random.randint(key_c, (N_REQ,), 0, ROWS_PER_INDEX)
    places = jnp.arange(N_REQ) * ROWS_PER_INDEX + longest
    return lengths.at[places].set(CTX).astype(jnp.int32)


def draw_row_adapter_index(key, part):
    key_h, key_n, key_t, key_p, key_f, key_a, key_b = jax.random.split(key, 7)
    slot_total = N_REQ * CAP
    heat = jax.random.randint(key_h, (N_REQ,), 0, 3)
    leader = jax.random.randint(key_t, (), 0, N_REQ)
    owner_of_slot = jnp.arange(slot_total) // CAP
    noise = jax.random.randint(key_n, (N_REQ, N_REQ), 0, 3)

    def one_block(noise_row, block_key):
        key_x, key_y = jax.random.split(block_key)
        level = heat[owner_of_slot] + noise_row[owner_of_slot] + 8 * (owner_of_slot == leader).astype(jnp.int32)
        score = level * slot_total + jax.random.permutation(key_x, slot_total)
        picked = lax.top_k(score, ROWS_PER_INDEX)[1]
        owners = picked // CAP
        return owners[jax.random.permutation(key_y, ROWS_PER_INDEX)]
    owners = jax.vmap(one_block)(noise, jax.random.split(key_p, N_REQ)).reshape(REQUEST_ROWS)
    favorite = jax.random.randint(key_f, (N_REQ,), 0, ADP_REQ)
    lower = jnp.minimum(jax.random.randint(key_a, (REQUEST_ROWS,), 0, ADP_REQ), jax.random.randint(key_b, (REQUEST_ROWS,), 0, ADP_REQ))
    local = (lower + favorite[owners]) % ADP_REQ
    return (owners * ADP_REQ + local).astype(jnp.int32)


def levels(own_key, shape, pieces, least, largest):
    gain = 1.0
    for position, blocks in pieces:
        heights = jax.random.uniform(jax.random.fold_in(jax.random.fold_in(own_key, 6), position), (blocks,), jnp.float32, least / len(pieces), largest / len(pieces))
        gain = gain * jnp.repeat(jnp.exp(heights), shape[position] // blocks).reshape((-1,) + (1,) * (len(shape) - 1 - position))
    return gain


def normal_values(key, shape, spread, bound, shards=(), kind=jnp.bfloat16):
    entries = spread * jax.random.normal(key, shape, jnp.float32)
    if shards:
        entries = entries * levels(key, shape, shards, -0.22, 0.18)
    return jnp.clip(entries, -bound, bound).astype(kind)


def setup_inputs(seed: int = 0) -> dict:
    arg_keys = jax.random.split(jax.random.key(seed), 8)
    queries = draw_queries(jax.random.fold_in(arg_keys[7], 71), 0)
    key_cache = draw_key_cache(jax.random.fold_in(arg_keys[7], 71), 0)
    value_cache = normal_values(arg_keys[2], (REQUEST_ROWS, CTX, KV_HEADS * HEAD_DIM), 1.0, 5.0, ((0, 8), (2, 4)))
    lengths = draw_lengths(jax.random.fold_in(arg_keys[7], 71), 0)
    row_adapter_index = draw_row_adapter_index(jax.random.fold_in(arg_keys[7], 71), 0)
    down_weight = normal_values(arg_keys[5], (ADAPTER_TOTAL, MODEL_WIDTH, ADAPTER_RANK), MODEL_WIDTH ** -0.5, 0.0625, ((0, 8), (1, 4)))
    up_weight = normal_values(arg_keys[6], (ADAPTER_TOTAL, ADAPTER_RANK, MODEL_WIDTH), (ADAPTER_RANK // 4) ** -0.5, 1.5, ((0, 8), (2, 4)))
    return {"queries": queries, "key_cache": key_cache, "value_cache": value_cache, "lengths": lengths, "row_adapter_index": row_adapter_index, "down_weight": down_weight, "up_weight": up_weight}


def attend_block(block):
    query_rows, key_rows, value_rows, length_rows = block
    count = query_rows.shape[0]
    query_heads = query_rows.reshape(count, KV_HEADS, GROUP, HEAD_DIM).astype(jnp.float32)
    key_heads = key_rows.reshape(count, CTX, KV_HEADS, HEAD_DIM).astype(jnp.float32)
    value_heads = value_rows.reshape(count, CTX, KV_HEADS, HEAD_DIM).astype(jnp.float32)
    scores = jnp.einsum("rkgd,rckd->rkgc", query_heads, key_heads) * (HEAD_DIM ** -0.5)
    valid = jnp.arange(CTX)[None, :] < length_rows[:, None]
    scores = jnp.where(valid[:, None, None, :], scores, -jnp.inf)
    highest = jnp.max(scores, axis=3, keepdims=True)
    expo = jnp.exp(scores - highest)
    weights = (expo / jnp.sum(expo, axis=3, keepdims=True)).astype(jnp.bfloat16)
    mixed = jnp.einsum("rkgc,rckd->rkgd", weights.astype(jnp.float32), value_heads)
    return mixed.astype(jnp.bfloat16).reshape(count, MODEL_WIDTH)


def reference(queries, key_cache, value_cache, lengths, row_adapter_index, down_weight, up_weight):
    block_list = REQUEST_ROWS // ROWS_PER_INDEX
    width_kv = KV_HEADS * HEAD_DIM
    decode_attention = lax.map(attend_block, (queries.reshape(block_list, ROWS_PER_INDEX, MODEL_WIDTH),
                                  key_cache.reshape(block_list, ROWS_PER_INDEX, CTX, width_kv),
                                  value_cache.reshape(block_list, ROWS_PER_INDEX, CTX, width_kv),
                                  lengths.reshape(block_list, ROWS_PER_INDEX)))
    decode_attention = decode_attention.reshape(REQUEST_ROWS, MODEL_WIDTH)

    def apply_adapter_block(block):
        rows_in, incoming_index = block
        down_matrices = down_weight[incoming_index.astype(jnp.int32)].astype(jnp.float32)
        shrink = jnp.einsum("bd,bdr->br", rows_in.astype(jnp.float32), down_matrices).astype(jnp.bfloat16)
        up_matrices = up_weight[incoming_index.astype(jnp.int32)].astype(jnp.float32)
        return jnp.einsum("br,bre->be", shrink.astype(jnp.float32), up_matrices).astype(jnp.bfloat16)

    low_rank_term = lax.map(apply_adapter_block, (decode_attention.reshape(block_list, ROWS_PER_INDEX, MODEL_WIDTH), row_adapter_index.reshape(block_list, ROWS_PER_INDEX)))
    return decode_attention, low_rank_term.reshape(REQUEST_ROWS, MODEL_WIDTH)
```

```python
import functools

import jax
import jax.numpy as jnp
from jax import lax
from jax.experimental import pallas as pl
from jax.experimental.pallas import tpu as pltpu
from jax.sharding import PartitionSpec as P

HEAD_DIM = 128
CAP = 8
CTX = 64
GROUP = 8
RANK = 64
SUB = 8
BLOCK = 16
MESH = pl.DeviceIdType.MESH
F32 = jnp.float32
BF16 = jnp.bfloat16
NT = (((1,), (1,)), ((), ()))
NN = (((1,), (0,)), ((), ()))
TN = (((0,), (0,)), ((), ()))


def dot(a, b, dims=NN):
    return lax.dot_general(a, b, dims, preferred_element_type=F32)


def swap_halves(x):
    return jnp.concatenate([x[:, RANK:], x[:, :RANK]], axis=1)


def ranks_in_block(onehot):
    rows = onehot.shape[1]
    before = lax.broadcasted_iota(jnp.int32, (rows, rows), 0)
    after = lax.broadcasted_iota(jnp.int32, (rows, rows), 1)
    earlier = jnp.where(before < after, 1.0, 0.0).astype(BF16)
    return dot(onehot.astype(BF16), earlier)


def to_blocks(x, n_req):
    half = x.shape[1] // 2
    out = []
    for o in range(n_req):
        tile = x[o * CAP : (o + 1) * CAP]
        out.append(jnp.concatenate([tile[:, :half], tile[:, half:]], axis=0).astype(BF16))
    return out


def from_blocks(blocks):
    n_req, _, half = blocks.shape
    wide = blocks.astype(F32)
    low = wide[:, :CAP].reshape(n_req * CAP, half)
    high = wide[:, CAP:].reshape(n_req * CAP, half)
    return jnp.concatenate([low, high], axis=1).astype(BF16)


def kernel(
    n_req, n_tp, adapters,
    q_hbm, k_hbm, v_hbm, lengths_ref, index_ref, down_hbm, up_hbm,
    attn_ref, out_ref,
    q, k, v, down, up, send1, recv1, send2, recv2, partial, peers, len_ref,
    load_sem, kv_sem, s1, r1, s2, r2, s3, r3,
):
    rows, width = q.shape
    slots = n_req * CAP
    kv_local = k.shape[1] // HEAD_DIM
    span = GROUP * HEAD_DIM
    parts = kv_local
    me = lax.axis_index("req")
    my_tp = lax.axis_index("tp")

    q_copy = pltpu.make_async_copy(q_hbm, q, load_sem.at[0])
    q_copy.start()
    n_blocks = rows // BLOCK
    kv_rows = BLOCK * CTX

    def kv_copies(b):
        at = pl.ds(pl.multiple_of(b * kv_rows, kv_rows), kv_rows)
        return (
            pltpu.make_async_copy(k_hbm.at[at], k.at[at], kv_sem.at[0, b]),
            pltpu.make_async_copy(v_hbm.at[at], v.at[at], kv_sem.at[1, b]),
        )

    for b in range(n_blocks):
        for copy in kv_copies(b):
            copy.start()
    down_copy = pltpu.make_async_copy(down_hbm, down, load_sem.at[1])
    down_copy.start()
    up_copy = pltpu.make_async_copy(up_hbm, up, load_sem.at[2])
    up_copy.start()

    barrier = pltpu.get_barrier_semaphore()
    req_to = [lax.rem(me + d, n_req) for d in range(n_req)]
    tp_to = [lax.rem(my_tp + d, n_tp) for d in range(n_tp)]
    for d in range(1, n_req):
        pl.semaphore_signal(barrier, inc=1, device_id=(req_to[d], my_tp), device_id_type=MESH)
    for d in range(1, n_tp):
        pl.semaphore_signal(barrier, inc=1, device_id=(me, tp_to[d]), device_id_type=MESH)

    index = index_ref[...]
    spread_index = jnp.broadcast_to(index[:, None, :], (n_req, CAP, rows)).reshape(slots, rows)
    slot_iota = lax.broadcasted_iota(jnp.int32, (slots, rows), 0)
    slot_rank = (slot_iota % CAP).astype(F32)
    owner_of_slot = slot_iota // CAP
    mine = jnp.broadcast_to(index_ref[pl.ds(me, 1), :], (slots, rows))
    to_owner = jnp.where(mine // adapters == owner_of_slot, 1.0, 0.0)
    pack = jnp.where(ranks_in_block(to_owner) == slot_rank, to_owner, 0.0).astype(BF16)
    to_me = jnp.where(spread_index // adapters == me, 1.0, 0.0)
    taken = jnp.where(ranks_in_block(to_me) == slot_rank, to_me, 0.0)
    local = (spread_index % adapters + 1).astype(F32)
    adapter = jnp.sum(taken * local, axis=1, keepdims=True).astype(jnp.int32) - 1

    row_r = lax.broadcasted_iota(jnp.int32, (rows, rows), 0)
    row_c = lax.broadcasted_iota(jnp.int32, (rows, rows), 1)
    len_row = jnp.broadcast_to(lengths_ref[...].astype(F32), (rows, rows))
    len_col = jnp.sum(jnp.where(row_r == row_c, len_row, 0.0), axis=1, keepdims=True)
    len_ref[...] = jnp.broadcast_to(len_col.astype(jnp.int32), len_ref.shape)

    q_copy.wait()
    keys = SUB * CTX
    place = lax.broadcasted_iota(jnp.int32, (SUB, keys), 1) - CTX * lax.broadcasted_iota(
        jnp.int32, (SUB, keys), 0
    )

    def exchange(m, d, src, dst, ssem, rsem):
        return pltpu.make_async_remote_copy(
            src_ref=src.at[m, req_to[d]],
            dst_ref=dst.at[m, me],
            send_sem=ssem.at[m, d],
            recv_sem=rsem.at[m, d],
            device_id=(req_to[d], my_tp),
            device_id_type=MESH,
        )

    for m in range(kv_local):
        cols = slice(m * HEAD_DIM, (m + 1) * HEAD_DIM)

        def attend(b, carry):
            if m == 0:
                for copy in kv_copies(b):
                    copy.wait()
            at = pl.ds(pl.multiple_of(b * BLOCK, BLOCK), BLOCK)
            q_block = q[at, m * span : (m + 1) * span].astype(F32)
            mixed = []
            for s in range(BLOCK // SUB):
                kv_at = pl.ds(pl.multiple_of(b * kv_rows + s * keys, keys), keys)
                q_rows = q_block[s * SUB : (s + 1) * SUB]
                q_heads = jnp.concatenate(
                    [q_rows[:, h * HEAD_DIM : (h + 1) * HEAD_DIM] for h in range(GROUP)], axis=0
                ).astype(BF16)
                scores = dot(q_heads, k[kv_at, cols], NT) * HEAD_DIM ** (-0.5)
                length = len_ref[pl.ds(pl.multiple_of(b * BLOCK + s * SUB, SUB), SUB), 0:1]
                live = jnp.logical_and(place >= 0, place < length)
                live = jnp.concatenate([live] * GROUP, axis=0)
                scores = jnp.where(live, scores, -jnp.inf)
                highest = jnp.max(scores, axis=1, keepdims=True)
                expo = jnp.exp(scores - highest)
                weights = (expo * (1.0 / jnp.sum(expo, axis=1, keepdims=True))).astype(BF16)
                mixed.append(dot(weights, v[kv_at, cols]))
            for h in range(GROUP):
                tile = jnp.concatenate([x[h * SUB : (h + 1) * SUB] for x in mixed], axis=0)
                first = m * span + h * HEAD_DIM
                attn_ref[at, first : first + HEAD_DIM] = tile.astype(BF16)
            return carry

        lax.fori_loop(0, n_blocks, attend, 0)
        packed = dot(pack, attn_ref[:, m * span : (m + 1) * span])
        for o, block in enumerate(to_blocks(packed, n_req)):
            send1[m, o] = block
        recv1[m, me] = send1[m, me]
        if m == 0:
            pl.semaphore_wait(barrier, n_req - 1 + n_tp - 1)
        for d in range(1, n_req):
            exchange(m, d, send1, recv1, s1, r1).start()

    tile_w = 4 * RANK
    lane = lax.broadcasted_iota(jnp.int32, (slots, 2 * RANK), 1)
    odd = jnp.where(lane >= RANK, 1, 0)
    pair_of_lane = adapter - odd

    down_copy.wait()
    total = jnp.zeros((slots, 2 * RANK), F32)
    for m in range(parts):
        for d in range(1, n_req):
            exchange(m, d, send1, recv1, s1, r1).wait_recv()
        x = from_blocks(recv1[m])

        def shrink_tile(c, acc):
            at = pl.ds(pl.multiple_of(c * tile_w, tile_w), tile_w)
            both = dot(x, down[at, m * span : (m + 1) * span], NT)
            for i in range(2):
                keep = pair_of_lane == 4 * c + 2 * i
                acc = acc + jnp.where(keep, both[:, i * 2 * RANK : (i + 1) * 2 * RANK], 0.0)
            return acc

        total = lax.fori_loop(0, adapters * RANK // tile_w, shrink_tile, total)

    folded = total + swap_halves(total)
    low = lax.broadcasted_iota(jnp.int32, (slots // 2, 2 * RANK), 1) < RANK
    partial[...] = jnp.where(low, folded[: slots // 2], folded[slots // 2 :])

    def share(d):
        return pltpu.make_async_remote_copy(
            src_ref=partial,
            dst_ref=peers.at[d],
            send_sem=s3.at[d],
            recv_sem=r3.at[d],
            device_id=(me, tp_to[d]),
            device_id_type=MESH,
        )

    for d in range(1, n_tp):
        share(d).start()
    shrink = partial[...]
    for d in range(1, n_tp):
        share(d).wait_recv()
        shrink = shrink + peers[d]
    swapped = swap_halves(shrink)
    shrink = jnp.concatenate([jnp.where(low, shrink, swapped), jnp.where(low, swapped, shrink)], axis=0)
    spread = jnp.concatenate(
        [jnp.where(pair_of_lane == 2 * j, shrink, 0.0).astype(BF16) for j in range(adapters // 2)],
        axis=1,
    )

    up_copy.wait()
    for m in range(parts):
        term = dot(spread, up[:, m * span : (m + 1) * span])
        for o, block in enumerate(to_blocks(term, n_req)):
            send2[m, o] = block
        recv2[m, me] = send2[m, me]
        for d in range(1, n_req):
            exchange(m, d, send2, recv2, s2, r2).start()
    for m in range(parts):
        for d in range(1, n_req):
            exchange(m, d, send2, recv2, s2, r2).wait_recv()
        y = from_blocks(recv2[m])
        out_ref[:, m * span : (m + 1) * span] = dot(pack, y, TN).astype(BF16)

    for m in range(parts):
        for d in range(1, n_req):
            exchange(m, d, send1, recv1, s1, r1).wait_send()
            exchange(m, d, send2, recv2, s2, r2).wait_send()
    for d in range(1, n_tp):
        share(d).wait_send()


def on_device(n_req, n_tp, queries, key_cache, value_cache, lengths, index, down_weight, up_weight):
    rows, width = queries.shape
    kv_width = key_cache.shape[2]
    kv_local = kv_width // HEAD_DIM
    adapters = down_weight.shape[0]
    slots = n_req * CAP
    half = GROUP * HEAD_DIM // 2
    out = jax.ShapeDtypeStruct((rows, width), BF16)
    hbm = pl.BlockSpec(memory_space=pl.ANY)
    vmem = pl.BlockSpec(memory_space=pltpu.VMEM)
    blocks = pltpu.VMEM((kv_local, n_req, 2 * CAP, half), BF16)
    dma = pltpu.SemaphoreType.DMA
    return pl.pallas_call(
        functools.partial(kernel, n_req, n_tp, adapters),
        out_shape=(out, out),
        in_specs=[hbm, hbm, hbm, vmem, vmem, hbm, hbm],
        out_specs=(vmem, vmem),
        scratch_shapes=[
            pltpu.VMEM((rows, width), BF16),
            pltpu.VMEM((rows * CTX, kv_width), BF16),
            pltpu.VMEM((rows * CTX, kv_width), BF16),
            pltpu.VMEM((adapters * RANK, width), BF16),
            pltpu.VMEM((adapters * RANK, width), BF16),
            blocks, blocks, blocks, blocks,
            pltpu.VMEM((slots // 2, 2 * RANK), F32),
            pltpu.VMEM((n_tp, slots // 2, 2 * RANK), F32),
            pltpu.VMEM((rows, HEAD_DIM), jnp.int32),
            dma((3,)),
            dma((2, rows // BLOCK)),
            dma((kv_local, n_req)), dma((kv_local, n_req)),
            dma((kv_local, n_req)), dma((kv_local, n_req)),
            dma((n_tp,)), dma((n_tp,)),
        ],
        compiler_params=pltpu.CompilerParams(
            collective_id=0, has_side_effects=True, vmem_limit_bytes=48 * 2**20
        ),
        cost_estimate=pl.CostEstimate(
            flops=4 * slots * adapters * RANK * width, bytes_accessed=22 * 2**20, transcendentals=0
        ),
    )(
        queries,
        key_cache.reshape(rows * CTX, kv_width),
        value_cache.reshape(rows * CTX, kv_width),
        lengths.reshape(1, rows),
        index.reshape(n_req, rows),
        jnp.swapaxes(down_weight, 1, 2).reshape(adapters * RANK, width),
        up_weight.reshape(adapters * RANK, width),
    )


def solution(mesh):
    in_specs = (
        P("req", "tp"),
        P("req", None, "tp"),
        P("req", None, "tp"),
        P("req"),
        P(),
        P("req", "tp", None),
        P("req", None, "tp"),
    )
    out_specs = (P("req", "tp"), P("req", "tp"))
    return jax.shard_map(
        functools.partial(on_device, mesh.shape["req"], mesh.shape["tp"]),
        mesh=mesh, in_specs=in_specs, out_specs=out_specs, check_vma=False,
    )
```

```python
import functools

import jax
import jax.numpy as jnp
from jax import lax
from jax.experimental import pallas as pl
from jax.experimental.pallas import tpu as pltpu
from jax.sharding import PartitionSpec as P

HEAD_DIM = 128
CAP = 8
CTX = 64
GROUP = 8
RANK = 64
SUB = 8
BLOCK = 16
MESH = pl.DeviceIdType.MESH
F32 = jnp.float32
BF16 = jnp.bfloat16
NT = (((1,), (1,)), ((), ()))
NN = (((1,), (0,)), ((), ()))
TN = (((0,), (0,)), ((), ()))


def dot(a, b, dims=NN):
    return lax.dot_general(a, b, dims, preferred_element_type=F32)


def swap_halves(x):
    return jnp.concatenate([x[:, RANK:], x[:, :RANK]], axis=1)


def ranks_in_block(onehot):
    rows = onehot.shape[1]
    before = lax.broadcasted_iota(jnp.int32, (rows, rows), 0)
    after = lax.broadcasted_iota(jnp.int32, (rows, rows), 1)
    earlier = jnp.where(before < after, 1.0, 0.0).astype(BF16)
    return dot(onehot.astype(BF16), earlier)


def to_blocks(x, n_req):
    half = x.shape[1] // 2
    out = []
    for o in range(n_req):
        tile = x[o * CAP : (o + 1) * CAP]
        out.append(jnp.concatenate([tile[:, :half], tile[:, half:]], axis=0).astype(BF16))
    return out


def from_blocks(blocks):
    n_req, _, half = blocks.shape
    wide = blocks.astype(F32)
    low = wide[:, :CAP].reshape(n_req * CAP, half)
    high = wide[:, CAP:].reshape(n_req * CAP, half)
    return jnp.concatenate([low, high], axis=1).astype(BF16)


def kernel(
    n_req, n_tp, adapters,
    q_hbm, k_hbm, v_hbm, lengths_hbm, index_hbm, down_hbm, up_hbm,
    attn_ref, out_ref,
    q, k, v, down, up, send1, recv1, send2, recv2, partial, peers, len_ref, lengths_ref, index_ref,
    load_sem, kv_sem, s1, r1, s2, r2, s3, r3,
):
    rows, width = q.shape
    slots = n_req * CAP
    kv_local = k.shape[1] // HEAD_DIM
    span = GROUP * HEAD_DIM
    parts = kv_local
    me = lax.axis_index("req")
    my_tp = lax.axis_index("tp")

    index_copy = pltpu.make_async_copy(index_hbm, index_ref, load_sem.at[3])
    index_copy.start()
    lengths_copy = pltpu.make_async_copy(lengths_hbm, lengths_ref, load_sem.at[4])
    lengths_copy.start()
    q_copy = pltpu.make_async_copy(q_hbm, q, load_sem.at[0])
    q_copy.start()
    n_blocks = rows // BLOCK
    kv_rows = BLOCK * CTX

    def kv_copies(b):
        at = pl.ds(pl.multiple_of(b * kv_rows, kv_rows), kv_rows)
        return (
            pltpu.make_async_copy(k_hbm.at[at], k.at[at], kv_sem.at[0, b]),
            pltpu.make_async_copy(v_hbm.at[at], v.at[at], kv_sem.at[1, b]),
        )

    for b in range(n_blocks):
        for copy in kv_copies(b):
            copy.start()
    down_copy = pltpu.make_async_copy(down_hbm, down, load_sem.at[1])
    down_copy.start()
    up_copy = pltpu.make_async_copy(up_hbm, up, load_sem.at[2])

    barrier = pltpu.get_barrier_semaphore()
    req_to = [lax.rem(me + d, n_req) for d in range(n_req)]
    tp_to = [lax.rem(my_tp + d, n_tp) for d in range(n_tp)]
    for d in range(1, n_req):
        pl.semaphore_signal(barrier, inc=1, device_id=(req_to[d], my_tp), device_id_type=MESH)
    for d in range(1, n_tp):
        pl.semaphore_signal(barrier, inc=1, device_id=(me, tp_to[d]), device_id_type=MESH)

    index_copy.wait()
    lengths_copy.wait()
    spread_index = jnp.concatenate(
        [
            jnp.broadcast_to(index_ref[:, p * rows : (p + 1) * rows], (CAP, rows))
            for p in range(n_req)
        ],
        axis=0,
    )
    slot_iota = lax.broadcasted_iota(jnp.int32, (slots, rows), 0)
    slot_rank = (slot_iota % CAP).astype(F32)
    owner_of_slot = slot_iota // CAP
    mine = spread_index[:CAP]
    for p in range(1, n_req):
        mine = jnp.where(me == p, spread_index[p * CAP : (p + 1) * CAP], mine)
    mine = jnp.concatenate([mine] * n_req, axis=0)
    to_owner = jnp.where(mine // adapters == owner_of_slot, 1.0, 0.0)
    pack = jnp.where(ranks_in_block(to_owner) == slot_rank, to_owner, 0.0).astype(BF16)
    to_me = jnp.where(spread_index // adapters == me, 1.0, 0.0)
    taken = jnp.where(ranks_in_block(to_me) == slot_rank, to_me, 0.0)
    local = (spread_index % adapters + 1).astype(F32)
    adapter = jnp.sum(taken * local, axis=1, keepdims=True).astype(jnp.int32) - 1

    row_r = lax.broadcasted_iota(jnp.int32, (rows, rows), 0)
    row_c = lax.broadcasted_iota(jnp.int32, (rows, rows), 1)
    len_row = jnp.broadcast_to(lengths_ref[...].astype(F32), (rows, rows))
    len_col = jnp.sum(jnp.where(row_r == row_c, len_row, 0.0), axis=1, keepdims=True)
    len_ref[...] = jnp.broadcast_to(len_col.astype(jnp.int32), len_ref.shape)

    q_copy.wait()
    keys = SUB * CTX
    place = lax.broadcasted_iota(jnp.int32, (SUB, keys), 1) - CTX * lax.broadcasted_iota(
        jnp.int32, (SUB, keys), 0
    )

    def exchange(m, d, src, dst, ssem, rsem):
        return pltpu.make_async_remote_copy(
            src_ref=src.at[m, req_to[d]],
            dst_ref=dst.at[m, me],
            send_sem=ssem.at[m, d],
            recv_sem=rsem.at[m, d],
            device_id=(req_to[d], my_tp),
            device_id_type=MESH,
        )

    for m in range(kv_local):
        cols = slice(m * HEAD_DIM, (m + 1) * HEAD_DIM)

        def attend(b, carry):
            if m == 0:
                for copy in kv_copies(b):
                    copy.wait()
            at = pl.ds(pl.multiple_of(b * BLOCK, BLOCK), BLOCK)
            q_block = q[at, m * span : (m + 1) * span].astype(F32)
            mixed = []
            for s in range(BLOCK // SUB):
                kv_at = pl.ds(pl.multiple_of(b * kv_rows + s * keys, keys), keys)
                q_rows = q_block[s * SUB : (s + 1) * SUB]
                q_heads = jnp.concatenate(
                    [q_rows[:, h * HEAD_DIM : (h + 1) * HEAD_DIM] for h in range(GROUP)], axis=0
                ).astype(BF16)
                scores = dot(q_heads, k[kv_at, cols], NT) * HEAD_DIM ** (-0.5)
                length = len_ref[pl.ds(pl.multiple_of(b * BLOCK + s * SUB, SUB), SUB), 0:1]
                live = jnp.logical_and(place >= 0, place < length)
                live = jnp.concatenate([live] * GROUP, axis=0)
                scores = jnp.where(live, scores, -jnp.inf)
                highest = jnp.max(scores, axis=1, keepdims=True)
                expo = jnp.exp(scores - highest)
                weights = (expo * (1.0 / jnp.sum(expo, axis=1, keepdims=True))).astype(BF16)
                mixed.append(dot(weights, v[kv_at, cols]))
            for h in range(GROUP):
                tile = jnp.concatenate([x[h * SUB : (h + 1) * SUB] for x in mixed], axis=0)
                first = m * span + h * HEAD_DIM
                attn_ref[at, first : first + HEAD_DIM] = tile.astype(BF16)
            return carry

        lax.fori_loop(0, n_blocks, attend, 0, unroll=True)
        packed = dot(pack, attn_ref[:, m * span : (m + 1) * span])
        for o, block in enumerate(to_blocks(packed, n_req)):
            send1[m, o] = block
        recv1[m, me] = send1[m, me]
        if m == 0:
            pl.semaphore_wait(barrier, n_req - 1 + n_tp - 1)
        for d in range(1, n_req):
            exchange(m, d, send1, recv1, s1, r1).start()

    up_copy.start()
    tile_w = 4 * RANK
    lane = lax.broadcasted_iota(jnp.int32, (slots, 2 * RANK), 1)
    odd = jnp.where(lane >= RANK, 1, 0)
    pair_of_lane = adapter - odd

    down_copy.wait()
    total = jnp.zeros((slots, 2 * RANK), F32)
    for m in range(parts):
        for d in range(1, n_req):
            exchange(m, d, send1, recv1, s1, r1).wait_recv()
        x = from_blocks(recv1[m])

        def shrink_tile(c, acc):
            at = pl.ds(pl.multiple_of(c * tile_w, tile_w), tile_w)
            both = dot(x, down[at, m * span : (m + 1) * span], NT)
            for i in range(2):
                keep = pair_of_lane == 4 * c + 2 * i
                acc = acc + jnp.where(keep, both[:, i * 2 * RANK : (i + 1) * 2 * RANK], 0.0)
            return acc

        total = lax.fori_loop(0, adapters * RANK // tile_w, shrink_tile, total, unroll=True)

    folded = total + swap_halves(total)
    low = lax.broadcasted_iota(jnp.int32, (slots // 2, 2 * RANK), 1) < RANK
    partial[...] = jnp.where(low, folded[: slots // 2], folded[slots // 2 :])

    def share(d):
        return pltpu.make_async_remote_copy(
            src_ref=partial,
            dst_ref=peers.at[d],
            send_sem=s3.at[d],
            recv_sem=r3.at[d],
            device_id=(me, tp_to[d]),
            device_id_type=MESH,
        )

    for d in range(1, n_tp):
        share(d).start()
    shrink = partial[...]
    for d in range(1, n_tp):
        share(d).wait_recv()
        shrink = shrink + peers[d]
    swapped = swap_halves(shrink)
    shrink = jnp.concatenate([jnp.where(low, shrink, swapped), jnp.where(low, swapped, shrink)], axis=0)
    spread = jnp.concatenate(
        [jnp.where(pair_of_lane == 2 * j, shrink, 0.0).astype(BF16) for j in range(adapters // 2)],
        axis=1,
    )

    up_copy.wait()
    for m in range(parts):
        term = dot(spread, up[:, m * span : (m + 1) * span])
        for o, block in enumerate(to_blocks(term, n_req)):
            send2[m, o] = block
        recv2[m, me] = send2[m, me]
        for d in range(1, n_req):
            exchange(m, d, send2, recv2, s2, r2).start()
    for m in range(parts):
        for d in range(1, n_req):
            exchange(m, d, send2, recv2, s2, r2).wait_recv()
        y = from_blocks(recv2[m])
        out_ref[:, m * span : (m + 1) * span] = dot(pack, y, TN).astype(BF16)

    for m in range(parts):
        for d in range(1, n_req):
            exchange(m, d, send1, recv1, s1, r1).wait_send()
            exchange(m, d, send2, recv2, s2, r2).wait_send()
    for d in range(1, n_tp):
        share(d).wait_send()


def on_device(n_req, n_tp, queries, key_cache, value_cache, lengths, index, down_weight, up_weight):
    rows, width = queries.shape
    kv_width = key_cache.shape[2]
    kv_local = kv_width // HEAD_DIM
    adapters = down_weight.shape[0]
    slots = n_req * CAP
    half = GROUP * HEAD_DIM // 2
    out = jax.ShapeDtypeStruct((rows, width), BF16)
    hbm = pl.BlockSpec(memory_space=pl.ANY)
    vmem = pl.BlockSpec(memory_space=pltpu.VMEM)
    blocks = pltpu.VMEM((kv_local, n_req, 2 * CAP, half), BF16)
    dma = pltpu.SemaphoreType.DMA
    return pl.pallas_call(
        functools.partial(kernel, n_req, n_tp, adapters),
        out_shape=(out, out),
        in_specs=[hbm] * 7,
        out_specs=(vmem, vmem),
        scratch_shapes=[
            pltpu.VMEM((rows, width), BF16),
            pltpu.VMEM((rows * CTX, kv_width), BF16),
            pltpu.VMEM((rows * CTX, kv_width), BF16),
            pltpu.VMEM((adapters * RANK, width), BF16),
            pltpu.VMEM((adapters * RANK, width), BF16),
            blocks, blocks, blocks, blocks,
            pltpu.VMEM((slots // 2, 2 * RANK), F32),
            pltpu.VMEM((n_tp, slots // 2, 2 * RANK), F32),
            pltpu.VMEM((rows, HEAD_DIM), jnp.int32),
            pltpu.VMEM((1, rows), jnp.int32),
            pltpu.VMEM((1, n_req * rows), jnp.int32),
            dma((5,)),
            dma((2, rows // BLOCK)),
            dma((kv_local, n_req)), dma((kv_local, n_req)),
            dma((kv_local, n_req)), dma((kv_local, n_req)),
            dma((n_tp,)), dma((n_tp,)),
        ],
        compiler_params=pltpu.CompilerParams(
            collective_id=0, has_side_effects=True, vmem_limit_bytes=63 * 2**20
        ),
        cost_estimate=pl.CostEstimate(
            flops=4 * slots * adapters * RANK * width, bytes_accessed=22 * 2**20, transcendentals=0
        ),
    )(
        queries,
        key_cache.reshape(rows * CTX, kv_width),
        value_cache.reshape(rows * CTX, kv_width),
        lengths.reshape(1, rows),
        index.reshape(1, n_req * rows),
        jnp.swapaxes(down_weight, 1, 2).reshape(adapters * RANK, width),
        up_weight.reshape(adapters * RANK, width),
    )


def solution(mesh):
    in_specs = (
        P("req", "tp"),
        P("req", None, "tp"),
        P("req", None, "tp"),
        P("req"),
        P(),
        P("req", "tp", None),
        P("req", None, "tp"),
    )
    out_specs = (P("req", "tp"), P("req", "tp"))
    return jax.shard_map(
        functools.partial(on_device, mesh.shape["req"], mesh.shape["tp"]),
        mesh=mesh, in_specs=in_specs, out_specs=out_specs, check_vma=False,
    )
```
